128 devices in a mesh: shot: 16 (over y_hi, x, core), slab: 8 (over y_lo, z).
Axes of the slice: x: 4, y: 4 (y_hi: 2, y_lo: 2; y = y_hi * 2 + y_lo), z: 4, core: 2. Of those that a mesh axis runs over, the one named last changes fastest.
Arguments:
- gradient: float32 [16, 128, 64, 256], P('shot', 'slab'), may hold values from -6 to 6
- illumination: float32 [16, 128, 64, 256], P('shot', 'slab'), may hold values from 0.5 to 4
- u_prev: float32 [16, 128, 64, 256], P('shot', 'slab'), may hold values from -6 to 6
- u_cur: float32 [16, 128, 64, 256], P('shot', 'slab'), may hold values from -6 to 6
- velocity: float32 [4, 128, 64, 256], P(None, 'slab'), may hold values from 2.5 to 4
- offsets: int32 [16], P('shot'), may hold values from 0 to 24
Outputs:
- new_model: float32 [4, 128, 64, 256], P(None, 'slab')
- wavefield: float32 [16, 128, 64, 256], P('shot', 'slab')
The draws below stay inside these ranges and needn't reach their ends.
Inputs may be any that keep to these rules, and one draw needn't show every extreme that they name: Shot s's aperture covers model slabs offsets[s] to offsets[s] + 128 / 16 - 1.
All inputs are finite; a program needn't handle non-finite values.
Results may differ from the reference program's by a relative error of at most 0.0003.
Values sent between devices are 32-bit elements; how exact they have to be, the bound alone decides.
No kernel may reach another device: no remote copies, remote signals or barrier semaphores. Data moves between devices by JAX's collectives and lax.ppermute only.
A program may use at most 128 MiB of HBM per device.

```python
import math
import jax
import jax.numpy as jnp
import numpy as np
from jax import lax

SX = 16
AY = 64
NZ = 256
SPAN = 4
NA = 128
NS = 32
SHOTS = 16
N_SLAB = 8


def with_ends(array, own_key, least, largest):
    place = [jax.random.randint(jax.random.fold_in(own_key, axis), (), 0, length) for axis, length in enumerate(array.shape)]
    widest = array.shape.index(max(array.shape))
    neighbour = place[:widest] + [(place[widest] + 1) % array.shape[widest]] + place[widest + 1:]
    return array.at[tuple(place)].set(least).at[tuple(neighbour)].set(largest)


def block_levels(own_key, shape, cuts, least, top_value):
    def one(axis_at, shards_of):
        draws = jax.random.uniform(jax.random.fold_in(jax.random.fold_in(own_key, 6), axis_at), (shards_of,), jnp.float32, least / len(cuts), top_value / len(cuts))
        return jnp.repeat(jnp.exp(draws), shape[axis_at] // shards_of).reshape((-1,) + (1,) * (len(shape) - axis_at - 1))

    factor_of = one(*cuts[0])
    for cut in cuts[1:]:
        factor_of = factor_of * one(*cut)
    return factor_of


def rank_bounds(number_of, lean):
    loads = [(1 << 20) // math.isqrt(rank ** lean) + 1 for rank in range(1, number_of + 1)]
    deviation = 1 + sum(loads) // (1 << 30)
    return np.cumsum(np.array([max(1, weight // deviation) for weight in loads]))


def skewed_ids(stream_key, extent, count, slope):
    grid = rank_bounds(count, slope)
    lot = jax.random.randint(jax.random.fold_in(stream_key, 1), extent, 0, int(grid[count - 1]))
    rank = jnp.searchsorted(jnp.asarray(grid, jnp.int32), lot, side="right")
    return jax.random.permutation(jax.random.fold_in(stream_key, 2), count)[rank].astype(jnp.int32)


def normal_values(own_key, dims, width, bound, pieces=(), dtype=jnp.bfloat16):
    array = width * jax.random.normal(own_key, dims, jnp.float32)
    if pieces:
        array = array * block_levels(own_key, dims, pieces, -0.22, 0.18)
    return jnp.clip(array, -bound, bound).astype(dtype)


def setup_inputs(seed: int = 0) -> dict:
    seeds = jax.random.split(jax.random.key(seed), 7)
    gradient = normal_values(seeds[0], (SHOTS, NA, AY, NZ), 0.5, 6.0, ((0, 16), (1, 8)), jnp.float32)
    illumination = jnp.clip(jnp.exp(math.log(4.0) - 2.0794415 * jax.random.uniform(seeds[1], (SHOTS, NA, AY, NZ), jnp.float32) ** block_levels(seeds[1], (SHOTS, NA, AY, NZ), ((0, 16), (1, 8)), -0.2, 0.2)), 0.5, 4.0)
    u_prev = normal_values(seeds[2], (SHOTS, NA, AY, NZ), 1.0, 6.0, ((0, 16), (1, 8)), jnp.float32)
    u_cur = normal_values(seeds[3], (SHOTS, NA, AY, NZ), 1.0, 6.0, ((0, 16), (1, 8)), jnp.float32)
    velocity = jnp.clip(2.5 + 1.5 * jax.random.uniform(seeds[4], (SPAN, NA, AY, NZ), jnp.float32) ** block_levels(seeds[4], (SPAN, NA, AY, NZ), ((1, 8),), -0.2, 0.2), 2.5, 4.0)
    offsets = with_ends(skewed_ids(seeds[5], (SHOTS,), NS - N_SLAB + 1, 2), jax.random.fold_in(seeds[5], 3), 0, NS - N_SLAB).astype(jnp.int32)
    return dict(gradient=gradient, illumination=illumination, u_prev=u_prev, u_cur=u_cur, velocity=velocity, offsets=offsets)


STENCIL = (-205.0 / 72.0, 8.0 / 5.0, -1.0 / 5.0, 8.0 / 315.0, -1.0 / 560.0)
RATE = 0.2
COURANT = 0.11


def laplace(field):
    padded = jnp.pad(field, 4)
    sizes = field.shape
    total = 3.0 * STENCIL[0] * field
    for reach in range(1, 5):
        along = padded[4 + reach:4 + reach + sizes[0], 4:4 + sizes[1], 4:4 + sizes[2]] + padded[4 - reach:4 - reach + sizes[0], 4:4 + sizes[1], 4:4 + sizes[2]]
        across = padded[4:4 + sizes[0], 4 + reach:4 + reach + sizes[1], 4:4 + sizes[2]] + padded[4:4 + sizes[0], 4 - reach:4 - reach + sizes[1], 4:4 + sizes[2]]
        downward = padded[4:4 + sizes[0], 4:4 + sizes[1], 4 + reach:4 + reach + sizes[2]] + padded[4:4 + sizes[0], 4:4 + sizes[1], 4 - reach:4 - reach + sizes[2]]
        total = total + STENCIL[reach] * (along + across + downward)
    return total


def reference(gradient, illumination, u_prev, u_cur, velocity, offsets):
    flat = velocity.reshape(SPAN * NA, AY, NZ)
    zero = jnp.int32(0)

    def add_shot(carry, item):
        grad_sum, illum_sum = carry
        grad_one, illum_one, offset = item
        start = (offset * SX).astype(jnp.int32)
        window = lax.dynamic_slice(grad_sum, (start, zero, zero), (NA, AY, NZ))
        grad_sum = lax.dynamic_update_slice(grad_sum, window + grad_one, (start, zero, zero))
        window = lax.dynamic_slice(illum_sum, (start, zero, zero), (NA, AY, NZ))
        illum_sum = lax.dynamic_update_slice(illum_sum, window + illum_one, (start, zero, zero))
        return (grad_sum, illum_sum), None

    empty = jnp.zeros((SPAN * NA, AY, NZ), jnp.float32)
    (grad_sum, illum_sum), _ = lax.scan(add_shot, (empty, empty), (gradient, illumination, offsets))
    updated = flat - RATE * grad_sum / (illum_sum + 1.0)

    def advance(item):
        previous, current, offset = item
        start = (offset * SX).astype(jnp.int32)
        local = lax.dynamic_slice(updated, (start, zero, zero), (NA, AY, NZ))
        squared = (local * COURANT) ** 2
        first = 2.0 * current - previous + squared * laplace(current)
        return 2.0 * first - current + squared * laplace(first)

    wavefield = lax.map(advance, (u_prev, u_cur, offsets))
    return updated.reshape(SPAN, NA, AY, NZ), wavefield
```

```python
import jax
import jax.numpy as jnp
from jax import lax
from jax.experimental import pallas as pl
from jax.experimental.pallas import tpu as pltpu
from jax.sharding import Mesh, PartitionSpec as P

STENCIL = (-205.0 / 72.0, 8.0 / 5.0, -1.0 / 5.0, 8.0 / 315.0, -1.0 / 560.0)
RATE = 0.2
COURANT = 0.11

AXES = ("yh", "x", "c", "yl", "z")
SIZES = {"yh": 2, "x": 4, "c": 2, "yl": 2, "z": 4}
SHOT = ("yh", "x", "c")
SLAB = ("yl", "z")
PLANE = ("yh", "x", "c", "yl")
PIECES = 32


def rotate(value, axis, steps):
    count = SIZES[axis]
    return lax.ppermute(value, axis, [(i, (i + steps) % count) for i in range(count)])


def halo(array, width):
    count, length = 8, array.shape[0]
    up = [(i, i + 1) for i in range(count - 1)]
    down = [(j, i) for i, j in up]
    before = lax.ppermute(array[length - width :], SLAB, up)
    after = lax.ppermute(array[:width], SLAB, down)
    return before, after


def laplace_rows(before, core, after):
    rows, widths, depths = core.shape
    extended = jnp.concatenate([before, core, after], axis=0)
    padded = jnp.pad(core, ((0, 0), (4, 4), (4, 4)))
    total = 3.0 * STENCIL[0] * core
    for reach in range(1, 5):
        along = extended[4 + reach : 4 + reach + rows] + extended[4 - reach : 4 - reach + rows]
        across = (
            padded[:, 4 + reach : 4 + reach + widths, 4 : 4 + depths]
            + padded[:, 4 - reach : 4 - reach + widths, 4 : 4 + depths]
        )
        downward = (
            padded[:, 4 : 4 + widths, 4 + reach : 4 + reach + depths]
            + padded[:, 4 : 4 + widths, 4 - reach : 4 - reach + depths]
        )
        total = total + STENCIL[reach] * (along + across + downward)
    return total


def gather_offsets(offsets):
    me = lax.axis_index(SHOT)
    value = jnp.where(jnp.arange(16, dtype=jnp.int32) == me, offsets[0], 0)
    value = value + rotate(value, "c", 1)
    value = value + rotate(value, "x", 1) + rotate(value, "x", 2) + rotate(value, "x", 3)
    return value + rotate(value, "yh", 1)


def bin_kernel(offs, items, own, one, two, three):
    outs = (own, one, two, three)
    for out in outs:
        out[...] = jnp.zeros_like(out)
    for item in range(PIECES):
        offset = offs[item // 2]
        place = lax.div(offset, 4) + item % 2
        shift = lax.rem(offset, 4)
        for k in range(4):

            @pl.when(shift == k)
            def _():
                outs[k][place] += items[item]


def put_in_bins(offs, items):
    shape = items.shape[1:]
    vmem = pl.BlockSpec(memory_space=pltpu.VMEM)
    return pl.pallas_call(
        bin_kernel,
        out_shape=[jax.ShapeDtypeStruct((8,) + shape, items.dtype)]
        + [jax.ShapeDtypeStruct((7,) + shape, items.dtype)] * 3,
        in_specs=[pl.BlockSpec(memory_space=pltpu.SMEM), vmem],
        out_specs=[vmem] * 4,
        cost_estimate=pl.CostEstimate(flops=1 << 18, bytes_accessed=1 << 21, transcendentals=0),
    )(offs, items)


def update_kernel(place, g0, g1, g2, g3, h0, h1, h2, h3, velocity, out, grad, illum):
    grad[...] = g0[...]
    illum[...] = h0[...]
    for k, g, h in ((1, g1, h1), (2, g2, h2), (3, g3, h3)):
        carry = (place[0] < k).astype(jnp.int32)
        grad[pl.ds(carry, 7)] += g[...]
        illum[pl.ds(carry, 7)] += h[...]
    out[...] = velocity[...] - RATE * grad[...] / (illum[...] + 1.0)


def update_model(place, grads, illums, velocity):
    vmem = pl.BlockSpec(memory_space=pltpu.VMEM)
    return pl.pallas_call(
        update_kernel,
        out_shape=jax.ShapeDtypeStruct(velocity.shape, velocity.dtype),
        in_specs=[pl.BlockSpec(memory_space=pltpu.SMEM)] + [vmem] * 9,
        out_specs=vmem,
        scratch_shapes=[pltpu.VMEM(velocity.shape, velocity.dtype)] * 2,
        cost_estimate=pl.CostEstimate(flops=1 << 19, bytes_accessed=1 << 22, transcendentals=0),
    )(place, *grads, *illums, velocity)


def pick_kernel(offs, place, n0, n1, n2, n3, out):
    refs = (n0, n1, n2, n3)
    for item in range(PIECES):
        offset = offs[item // 2]
        shift = lax.rem(offset, 4)
        slot = lax.div(offset, 4) + item % 2 + (place[0] + shift >= 4).astype(jnp.int32)
        for k in range(4):

            @pl.when(shift == k)
            def _():
                out[item] = refs[k][slot]


def pick(offs, place, news):
    shape = news[0].shape[1:]
    vmem = pl.BlockSpec(memory_space=pltpu.VMEM)
    smem = pl.BlockSpec(memory_space=pltpu.SMEM)
    return pl.pallas_call(
        pick_kernel,
        out_shape=jax.ShapeDtypeStruct((PIECES,) + shape, news[0].dtype),
        in_specs=[smem, smem] + [vmem] * 4,
        out_specs=vmem,
        cost_estimate=pl.CostEstimate(flops=1 << 18, bytes_accessed=1 << 21, transcendentals=0),
    )(offs, place, *news)


def on_device(gradient, illumination, u_prev, u_cur, velocity, offsets):
    shape = u_cur.shape[1:]
    u_prev, u_cur = u_prev[0], u_cur[0]
    yl, z = lax.axis_index("yl"), lax.axis_index("z")
    row = lax.axis_index(SHOT)
    place = z.astype(jnp.int32).reshape(1)
    offs = gather_offsets(offsets)

    halves = velocity.reshape(4, 16, 2, 32, 256)
    mine = lax.dynamic_slice(halves, (0, row, yl, 0, 0), (4, 1, 1, 32, 256)).reshape(4, 32, 256)
    send = lax.dynamic_slice(halves, (0, row, 1 - yl, 0, 0), (4, 1, 1, 32, 256)).reshape(4, 32, 256)
    other = rotate(send, "yl", 1)
    share = jnp.where(
        yl == 0, jnp.stack([mine, other], axis=1), jnp.stack([other, mine], axis=1)
    ).reshape(8, 32, 256)

    before, after = halo(u_cur, 4)
    first_lap = laplace_rows(before, u_cur, after)
    base = 2.0 * u_cur - u_prev

    grads = lax.all_to_all(gradient.reshape(PIECES, 32, 256), PLANE, 0, 0)
    illums = lax.all_to_all(illumination.reshape(PIECES, 32, 256), PLANE, 0, 0)
    grads = put_in_bins(offs, grads)
    illums = put_in_bins(offs, illums)
    grads = [grads[0]] + [rotate(grads[k], "z", k) for k in (1, 2, 3)]
    illums = [illums[0]] + [rotate(illums[k], "z", k) for k in (1, 2, 3)]
    new = update_model(place, grads, illums, share)

    news = [new] + [rotate(new, "z", -k) for k in (1, 2, 3)]
    items = pick(offs, place, news)
    local = lax.all_to_all(items, PLANE, 0, 0).reshape(shape)

    pairs = new.reshape(4, 2, 32, 256)
    keep = lax.dynamic_slice(pairs, (0, yl, 0, 0), (4, 1, 32, 256))
    give = lax.dynamic_slice(pairs, (0, 1 - yl, 0, 0), (4, 1, 32, 256))
    got = rotate(give, "yl", 1)
    whole = jnp.where(
        yl == 0, jnp.concatenate([keep, got], axis=1), jnp.concatenate([got, keep], axis=1)
    ).reshape(4, 1, 64, 256)
    new_model = lax.all_gather(whole, SHOT, axis=1, tiled=True)

    squared = (local * COURANT) ** 2
    one = base + squared * first_lap
    before, after = halo(one, 4)
    final = 2.0 * one - u_cur + squared * laplace_rows(before, one, after)
    return new_model, final[None]


def solution(mesh):
    fine = Mesh(mesh.devices.reshape(tuple(SIZES[a] for a in AXES)), AXES)
    field = P(SHOT, SLAB, None, None)
    model = P(None, SLAB, None, None)
    return jax.shard_map(
        on_device,
        mesh=fine,
        in_specs=(field, field, field, field, model, P(SHOT)),
        out_specs=(model, field),
        check_vma=False,
    )
```

```python
import jax
import jax.numpy as jnp
from jax import lax
from jax.experimental import pallas as pl
from jax.experimental.pallas import tpu as pltpu
from jax.sharding import Mesh, PartitionSpec as P

STENCIL = (-205.0 / 72.0, 8.0 / 5.0, -1.0 / 5.0, 8.0 / 315.0, -1.0 / 560.0)
RATE = 0.2
COURANT = 0.11

AXES = ("yh", "x", "c", "yl", "z")
SIZES = {"yh": 2, "x": 4, "c": 2, "yl": 2, "z": 4}
SHOT = ("yh", "x", "c")
SLAB = ("yl", "z")


def rotate(value, axis, steps):
    count = SIZES[axis]
    return lax.ppermute(value, axis, [(i, (i + steps) % count) for i in range(count)])


def halo(array, width):
    count, length = 8, array.shape[0]
    up = [(i, i + 1) for i in range(count - 1)]
    down = [(j, i) for i, j in up]
    before = lax.ppermute(array[length - width :], SLAB, up)
    after = lax.ppermute(array[:width], SLAB, down)
    return before, after


def laplace_rows(before, core, after):
    rows, widths, depths = core.shape
    extended = jnp.concatenate([before, core, after], axis=0)
    padded = jnp.pad(core, ((0, 0), (4, 4), (4, 4)))
    total = 3.0 * STENCIL[0] * core
    for reach in range(1, 5):
        along = extended[4 + reach : 4 + reach + rows] + extended[4 - reach : 4 - reach + rows]
        across = (
            padded[:, 4 + reach : 4 + reach + widths, 4 : 4 + depths]
            + padded[:, 4 - reach : 4 - reach + widths, 4 : 4 + depths]
        )
        downward = (
            padded[:, 4 : 4 + widths, 4 + reach : 4 + reach + depths]
            + padded[:, 4 : 4 + widths, 4 - reach : 4 - reach + depths]
        )
        total = total + STENCIL[reach] * (along + across + downward)
    return total


def gather_offsets(offsets):
    me = lax.axis_index(SHOT)
    value = jnp.where(jnp.arange(16, dtype=jnp.int32) == me, offsets[0], 0)
    value = value + rotate(value, "c", 1)
    value = value + rotate(value, "x", 1) + rotate(value, "x", 2) + rotate(value, "x", 3)
    return value + rotate(value, "yh", 1)


def model_kernel(offs, place, sent, near, far, items, z0, z1, z2, z3, grad, illum):
    z, yl = place[0], place[1]
    grad[...] = jnp.zeros_like(grad)
    illum[...] = jnp.zeros_like(illum)
    for shot in range(16):
        first = offs[shot]
        grad[pl.ds(first, 8)] += sent[8 * shot : 8 * shot + 8, :8]
        illum[pl.ds(first, 8)] += sent[8 * shot : 8 * shot + 8, 8:]
    for velocity, half in ((near, yl), (far, 1 - yl)):
        for k in range(4):
            for q in range(4):
                slab = 8 * q + 4 * half + lax.rem(z + 4 - k, 4)
                grad[slab] = velocity[k, q] - RATE * grad[slab] / (illum[slab] + 1.0)
    for shot in range(16):
        items[8 * shot : 8 * shot + 8] = grad[pl.ds(offs[shot], 8)]
    for k, out in enumerate((z0, z1, z2, z3)):
        there = lax.rem(z + k, 4)
        for q in range(4):
            for half in range(2):
                out[q, half] = grad[8 * q + 4 * half + there]


def update_model(offs, place, sent, near, far):
    vmem = pl.BlockSpec(memory_space=pltpu.VMEM)
    smem = pl.BlockSpec(memory_space=pltpu.SMEM)
    dtype = sent.dtype
    return pl.pallas_call(
        model_kernel,
        out_shape=[jax.ShapeDtypeStruct((128, 8, 256), dtype)]
        + [jax.ShapeDtypeStruct((4, 2, 8, 256), dtype)] * 4,
        in_specs=[smem, smem, vmem, vmem, vmem],
        out_specs=[vmem] * 5,
        scratch_shapes=[pltpu.VMEM((32, 8, 256), dtype)] * 2,
        cost_estimate=pl.CostEstimate(flops=1 << 20, bytes_accessed=1 << 22, transcendentals=0),
    )(offs, place, sent, near, far)


def row_kernel(place, near, far, out):
    z, yl = place[0], place[1]
    for parts, half in ((near, yl), (far, 1 - yl)):
        for k in range(4):
            block = 4 * half + lax.rem(z + 4 - k, 4)
            for q in range(4):
                out[q, block] = parts[k, q]


def order_row(place, near, far):
    vmem = pl.BlockSpec(memory_space=pltpu.VMEM)
    return pl.pallas_call(
        row_kernel,
        out_shape=jax.ShapeDtypeStruct((4, 8, 8, 256), near.dtype),
        in_specs=[pl.BlockSpec(memory_space=pltpu.SMEM), vmem, vmem],
        out_specs=vmem,
        cost_estimate=pl.CostEstimate(flops=0, bytes_accessed=1 << 19, transcendentals=0),
    )(place, near, far).reshape(4, 64, 256)


def place_kernel(rows, *refs):
    pieces, out, sems = refs[:16], refs[16], refs[17]
    copies = [
        pltpu.make_async_copy(piece, out.at[:, rows[i]], sems.at[i])
        for i, piece in enumerate(pieces)
    ]
    for copy in copies:
        copy.start()
    for copy in copies:
        copy.wait()


def place_rows(rows, pieces):
    hbm = pl.BlockSpec(memory_space=pl.ANY)
    return pl.pallas_call(
        place_kernel,
        out_shape=jax.ShapeDtypeStruct((4, 16) + pieces[0].shape[1:], pieces[0].dtype),
        in_specs=[pl.BlockSpec(memory_space=pltpu.SMEM)] + [hbm] * 16,
        out_specs=hbm,
        scratch_shapes=[pltpu.SemaphoreType.DMA((16,))],
        cost_estimate=pl.CostEstimate(flops=0, bytes_accessed=1 << 23, transcendentals=0),
    )(rows, *pieces)


def exchange(parts):
    yl = lax.axis_index("yl")
    parts = jnp.stack([parts[0]] + [rotate(parts[k], "z", k) for k in (1, 2, 3)])
    near = lax.dynamic_index_in_dim(parts, yl, 2, keepdims=False)
    far = lax.dynamic_index_in_dim(parts, 1 - yl, 2, keepdims=False)
    return near, rotate(far, "yl", 1)


def velocity_pieces(velocity):
    z = lax.axis_index("z")
    rows = lax.dynamic_index_in_dim(velocity, lax.axis_index(SHOT), 1, keepdims=False)
    rows = rows.reshape(4, 2, 4, 8, 256)
    return exchange([lax.dynamic_index_in_dim(rows, (z + k) % 4, 2, keepdims=False) for k in range(4)])


def gather_rows(own):
    yh, x, c = (lax.axis_index(a) for a in SHOT)
    found = [(own, 0, 0)] + [(rotate(own, "x", k), 0, k) for k in (1, 2, 3)]
    flipped = rotate(own, "yh", 1)
    found.append((flipped, 1, 0))
    found += [(rotate(flipped, "x", k), 1, k) for k in (1, 3)]
    found.append((rotate(found[2][0], "yh", 1), 1, 2))
    pieces, rows = [], []
    for value, dy, dx in found:
        base = ((yh + dy) % 2) * 8 + ((x - dx) % 4) * 2
        pieces += [value, rotate(value, "c", 1)]
        rows += [base + c, base + 1 - c]
    return place_rows(jnp.stack(rows).astype(jnp.int32), pieces)


def on_device(gradient, illumination, u_prev, u_cur, velocity, offsets):
    shape = u_cur.shape[1:]
    u_prev, u_cur = u_prev[0], u_cur[0]
    place = jnp.stack([lax.axis_index("z"), lax.axis_index("yl")]).astype(jnp.int32)

    sent = jnp.concatenate(
        [gradient.reshape(128, 8, 256), illumination.reshape(128, 8, 256)], axis=1
    )
    sent = lax.all_to_all(sent, AXES, 0, 0)

    offs = gather_offsets(offsets)
    near, far = velocity_pieces(velocity)
    before, after = halo(u_cur, 4)
    first_lap = laplace_rows(before, u_cur, after)
    base = 2.0 * u_cur - u_prev

    items, *parts = update_model(offs, place, sent, near, far)
    local = lax.all_to_all(items, AXES, 0, 0).reshape(shape)
    new_model = gather_rows(order_row(place, *exchange(parts)))

    squared = (local * COURANT) ** 2
    one = base + squared * first_lap
    before, after = halo(one, 4)
    final = 2.0 * one - u_cur + squared * laplace_rows(before, one, after)
    return new_model, final[None]


def solution(mesh):
    fine = Mesh(mesh.devices.reshape(tuple(SIZES[a] for a in AXES)), AXES)
    field = P(SHOT, SLAB, None, None)
    model = P(None, SLAB, None, None)
    return jax.shard_map(
        on_device,
        mesh=fine,
        in_specs=(field, field, field, field, model, P(SHOT)),
        out_specs=(model, field),
        check_vma=False,
    )
```

```python
import jax
import jax.numpy as jnp
import numpy as np
from jax import lax
from jax.experimental import pallas as pl
from jax.experimental.pallas import tpu as pltpu
from jax.sharding import Mesh, PartitionSpec as P

STENCIL = (-205.0 / 72.0, 8.0 / 5.0, -1.0 / 5.0, 8.0 / 315.0, -1.0 / 560.0)
RATE = 0.2
COURANT = 0.11

AXES = ("yh", "x", "c", "yl", "z")
SIZES = {"yh": 2, "x": 4, "c": 2, "yl": 2, "z": 4}
SHOT = ("yh", "x", "c")
SLAB = ("yl", "z")


def rotate(value, axis, steps):
    count = SIZES[axis]
    return lax.ppermute(value, axis, [(i, (i + steps) % count) for i in range(count)])


def banded(length, centre):
    matrix = centre * np.eye(length)
    for reach in range(1, 5):
        matrix += STENCIL[reach] * (np.eye(length, k=reach) + np.eye(length, k=-reach))
    return jnp.asarray(matrix, jnp.float32)


def halo(last, first):
    before = lax.ppermute(last, SLAB, [(i, (i + 1) % 8) for i in range(8)])
    after = lax.ppermute(first, SLAB, [((i + 1) % 8, i) for i in range(8)])
    return before, after


def dot(a, b):
    return jnp.dot(a, b, precision=lax.Precision.HIGHEST, preferred_element_type=jnp.float32)


def inside(field, depth, width, out):
    planes = field.shape[0]
    out[...] = dot(field[...].reshape(planes * 64, 256), depth[...]).reshape(planes, 64, 256)
    for i in range(planes):
        total = dot(width[...], field[i])
        for reach in range(1, 5):
            near = [field[j] for j in (i - reach, i + reach) if 0 <= j < planes]
            total += STENCIL[reach] * sum(near[1:], near[0])
        out[i] += total


def beyond(before, after, i, planes):
    if i < 4:
        return sum(STENCIL[reach] * before[4 + i - reach] for reach in range(i + 1, 5))
    low = planes - i
    return sum(STENCIL[reach] * after[reach - low] for reach in range(low, 5))


def first_kernel(previous, current, depth, width, base, lap):
    base[...] = 2.0 * current[...] - previous[...]
    inside(current, depth, width, lap)


def second_kernel(ends, back, base, lap, current, before, after, depth, width, most, squared, first, last, one):
    for plane in range(16):
        for block in range(8):
            for half in range(2):
                value = back[8 * plane + block, 8 * half : 8 * half + 8]
                at = (plane, slice(8 * block, 8 * block + 8), slice(128 * half, 128 * half + 128))
                squared[at] = (value * COURANT) ** 2
    for i in range(16):
        total = lap[i]
        if i < 4:
            total += jnp.where(ends[0] == 0, 0.0, beyond(before, after, i, 16))
        if i >= 12:
            total += jnp.where(ends[0] == 7, 0.0, beyond(before, after, i, 16))
        one[i] = base[i] + squared[i] * total
    first[...] = one[:4]
    last[...] = one[12:]
    inside(one, depth, width, most)
    for i in range(16):
        most[i] = 2.0 * one[i] - current[i] + squared[i] * most[i]


def third_kernel(ends, most, squared, before, after, out):
    out[4:12] = most[4:12]
    for i in (0, 1, 2, 3):
        out[i] = most[i] + squared[i] * jnp.where(ends[0] == 0, 0.0, beyond(before, after, i, 16))
    for i in (12, 13, 14, 15):
        out[i] = most[i] + squared[i] * jnp.where(ends[0] == 7, 0.0, beyond(before, after, i, 16))


def on_slab(kernel, outs, *args, scalars=0, scratch=(), bytes_accessed=8 << 20):
    vmem = pl.BlockSpec(memory_space=pltpu.VMEM)
    smem = pl.BlockSpec(memory_space=pltpu.SMEM)
    return pl.pallas_call(
        kernel,
        out_shape=[jax.ShapeDtypeStruct((planes, 64, 256), jnp.float32) for planes in outs],
        in_specs=[smem] * scalars + [vmem] * (len(args) - scalars),
        out_specs=[vmem] * len(outs),
        scratch_shapes=list(scratch),
        cost_estimate=pl.CostEstimate(flops=1 << 27, bytes_accessed=bytes_accessed, transcendentals=0),
    )(*args)


def pack_kernel(place, offset, gradient, illumination, velocity, out):
    for half in range(2):
        lanes = slice(128 * half, 128 * half + 128)
        out[:, 8 * half : 8 * half + 8] = gradient[:, :, lanes]
        out[:, 16 + 8 * half : 24 + 8 * half] = illumination[:, :, lanes]
    tile = velocity[...]
    upper = lax.broadcasted_iota(jnp.int32, tile.shape, 1) // 4
    out[:, 32:] = jnp.where(upper == place[2], tile, offset[0].astype(jnp.float32))


def pack(place, offsets, gradient, illumination, velocity):
    return pl.pallas_call(
        pack_kernel,
        grid_spec=pltpu.PrefetchScalarGridSpec(
            num_scalar_prefetch=2,
            grid=(1,),
            in_specs=[pl.BlockSpec((128, 8, 256), lambda i, place, offset: (0, 0, 0))] * 2
            + [pl.BlockSpec((None, 128, 8, 128), lambda i, place, offset: (place[0], 0, 0, place[1]))],
            out_specs=pl.BlockSpec((128, 40, 128), lambda i, place, offset: (0, 0, 0)),
        ),
        out_shape=jax.ShapeDtypeStruct((128, 40, 128), gradient.dtype),
        cost_estimate=pl.CostEstimate(flops=0, bytes_accessed=5 << 20, transcendentals=0),
    )(
        place,
        offsets,
        gradient.reshape(128, 8, 256),
        illumination.reshape(128, 8, 256),
        velocity.reshape(4, 128, 8, 256),
    )


def model_kernel(offs, sent, early, out, grad, illum):
    grad[...] = jnp.zeros_like(grad)
    illum[...] = jnp.zeros_like(illum)
    for shot in range(16):
        first = offs[shot]
        grad[pl.ds(first, 8)] += sent[8 * shot : 8 * shot + 8, :16]
        illum[pl.ds(first, 8)] += sent[8 * shot : 8 * shot + 8, 16:32]
    for pair in range(8):
        slabs, rows = pl.ds(8 * (pair // 2), 8), pl.ds(8 * (pair % 2), 8)
        low = sent[16 * pair : 16 * pair + 8, 32:]
        high = sent[16 * pair + 8 : 16 * pair + 16, 32:]
        velocity = jnp.where(lax.broadcasted_iota(jnp.int32, low.shape, 1) < 4, low, high)
        new = velocity - RATE * grad[slabs, rows] / (illum[slabs, rows] + 1.0)
        grad[slabs, rows] = new
        out[16 * pair : 16 * pair + 8, 16:] = new
        out[16 * pair + 8 : 16 * pair + 16, 16:] = new
    for shot in range(16):
        out[8 * shot : 8 * shot + 8, :16] = grad[pl.ds(offs[shot], 8)]


def update_model(offs, sent, early):
    vmem = pl.BlockSpec(memory_space=pltpu.VMEM)
    return pl.pallas_call(
        model_kernel,
        out_shape=jax.ShapeDtypeStruct((128, 24, 128), sent.dtype),
        in_specs=[pl.BlockSpec(memory_space=pltpu.SMEM), vmem, pl.BlockSpec(memory_space=pl.ANY)],
        out_specs=vmem,
        scratch_shapes=[pltpu.VMEM((32, 16, 128), sent.dtype)] * 2,
        cost_estimate=pl.CostEstimate(flops=1 << 20, bytes_accessed=4 << 20, transcendentals=0),
    )(offs, sent, early)


def place_kernel(spots, *refs):
    pieces, out, sems = refs[:16], refs[16], refs[17]
    copies = []
    for i, piece in enumerate(pieces):
        chip, core = spots[2 * i], spots[2 * i + 1]
        planes = pl.ds(pl.multiple_of(8 * core, 8), 8)
        lanes = pl.ds(pl.multiple_of(128 * lax.rem(chip, 2), 128), 128)
        target = out.at[lax.div(chip, 2), planes, :, lanes]
        copies.append(pltpu.make_async_copy(piece, target, sems.at[i]))
    for copy in copies:
        copy.start()
    for copy in copies:
        copy.wait()


def place_pieces(spots, pieces):
    vmem = pl.BlockSpec(memory_space=pltpu.VMEM)
    return pl.pallas_call(
        place_kernel,
        out_shape=jax.ShapeDtypeStruct((4, 16, 64, 256), pieces[0].dtype),
        in_specs=[pl.BlockSpec(memory_space=pltpu.SMEM)] + [vmem] * 16,
        out_specs=pl.BlockSpec(memory_space=pltpu.HBM),
        scratch_shapes=[pltpu.SemaphoreType.DMA((16,))],
        cost_estimate=pl.CostEstimate(flops=0, bytes_accessed=1 << 27, transcendentals=0),
    )(spots, *pieces)


def gather_model(own, between):
    yh, x, c = (lax.axis_index(a) for a in SHOT)
    first = [rotate(own, "x", k) for k in (1, 2, 3)] + [rotate(own, "yh", 1)]
    first, between = lax.optimization_barrier((first, between))
    found = [(own, 0, 0)] + [(first[k - 1], 0, k) for k in (1, 2, 3)]
    found.append((first[3], 1, 0))
    found += [(rotate(first[3], "x", k), 1, k) for k in (1, 3)]
    found.append((rotate(first[1], "yh", 1), 1, 2))
    pieces, spots = [], []
    for value, dy, dx in found:
        chip = ((yh + dy) % 2) * 4 + (x - dx) % 4
        pieces += [value, rotate(value, "c", 1)]
        spots += [chip, c, chip, 1 - c]
    return place_pieces(jnp.stack(spots).astype(jnp.int32), pieces), between


def on_device(gradient, illumination, u_prev, u_cur, velocity, offsets):
    u_prev, u_cur = u_prev[0], u_cur[0]
    yh, x, c = (lax.axis_index(a) for a in SHOT)
    place = jnp.stack([2 * yh + x // 2, x % 2, c, lax.axis_index(SLAB)]).astype(jnp.int32)

    sent = pack(place, offsets, gradient, illumination, velocity)
    sent = lax.all_to_all(sent, AXES, 0, 0)
    low, high = sent[0::16, 36, 0], sent[8::16, 32, 0]
    offs = jnp.stack([low, high], axis=1).reshape(16).astype(jnp.int32)

    back = lax.all_to_all(update_model(offs, sent, u_cur), AXES, 0, 0)

    depth, width = banded(256, 3.0 * STENCIL[0]), banded(64, 0.0)
    base, lap = on_slab(first_kernel, (16, 16), u_prev, u_cur, depth, width)
    around = halo(u_cur[12:], u_cur[:4])
    back, base, lap = lax.optimization_barrier((back, base, lap))

    own = lax.dynamic_slice(back, (64 * c, 16, 0), (64, 8, 128)).reshape(8, 64, 128)
    field = pltpu.VMEM((16, 64, 256), jnp.float32)
    step = on_slab(
        second_kernel, (16, 16, 4, 4), place[3:], back, base, lap, u_cur, *around, depth, width,
        scalars=1, scratch=[field],
    )
    new_model, (most, squared, first, last) = gather_model(own, tuple(step))
    around = halo(last, first)
    (final,) = on_slab(third_kernel, (16,), place[3:], most, squared, *around, scalars=1)
    return new_model, final[None]


def solution(mesh):
    fine = Mesh(mesh.devices.reshape(tuple(SIZES[a] for a in AXES)), AXES)
    field = P(SHOT, SLAB, None, None)
    model = P(None, SLAB, None, None)
    return jax.shard_map(
        on_device,
        mesh=fine,
        in_specs=(field, field, field, field, model, P(SHOT)),
        out_specs=(model, field),
        check_vma=False,
    )
```

```python
import functools

import jax
import jax.numpy as jnp
import numpy as np
from jax import lax
from jax.experimental import pallas as pl
from jax.experimental.pallas import tpu as pltpu
from jax.sharding import Mesh, PartitionSpec as P

STENCIL = (-205.0 / 72.0, 8.0 / 5.0, -1.0 / 5.0, 8.0 / 315.0, -1.0 / 560.0)
RATE = 0.2
COURANT = 0.11

AXES = ("yh", "x", "c", "yl", "z")
SIZES = {"yh": 2, "x": 4, "c": 2, "yl": 2, "z": 4}
SHOT = ("yh", "x", "c")
SLAB = ("yl", "z")


def rotate(value, axis, steps):
    count = SIZES[axis]
    return lax.ppermute(value, axis, [(i, (i + steps) % count) for i in range(count)])


def banded(length, centre):
    matrix = centre * np.eye(length)
    for reach in range(1, 5):
        matrix += STENCIL[reach] * (np.eye(length, k=reach) + np.eye(length, k=-reach))
    return jnp.asarray(matrix, jnp.float32)


def halo(last, first):
    before = lax.ppermute(last, SLAB, [(i, (i + 1) % 8) for i in range(8)])
    after = lax.ppermute(first, SLAB, [((i + 1) % 8, i) for i in range(8)])
    return before, after


def dot(a, b):
    return jnp.dot(a, b, precision=lax.Precision.HIGHEST, preferred_element_type=jnp.float32)


def inside(field, depth, width, out):
    planes = field.shape[0]
    out[...] = dot(field[...].reshape(planes * 64, 256), depth[...]).reshape(planes, 64, 256)
    for i in range(planes):
        total = dot(width[...], field[i])
        for reach in range(1, 5):
            near = [field[j] for j in (i - reach, i + reach) if 0 <= j < planes]
            total += STENCIL[reach] * sum(near[1:], near[0])
        out[i] += total


def beyond(before, after, i, planes):
    if i < 4:
        return sum(STENCIL[reach] * before[4 + i - reach] for reach in range(i + 1, 5))
    low = planes - i
    return sum(STENCIL[reach] * after[reach - low] for reach in range(low, 5))


def first_kernel(previous, current, depth, width, base, lap):
    inside(current, depth, width, lap)
    base[...] = 2.0 * current[...] - previous[...]


def second_kernel(back, base, lap, current, before, after, depth, width, most, squared, first, last, one):
    for plane in range(16):
        for block in range(8):
            for half in range(2):
                value = back[8 * plane + block, 8 * half : 8 * half + 8]
                at = (plane, slice(8 * block, 8 * block + 8), slice(128 * half, 128 * half + 128))
                squared[at] = (value * COURANT) ** 2
    for i in range(16):
        total = lap[i]
        if i < 4:
            total += jnp.where(lax.axis_index(SLAB) == 0, 0.0, beyond(before, after, i, 16))
        if i >= 12:
            total += jnp.where(lax.axis_index(SLAB) == 7, 0.0, beyond(before, after, i, 16))
        one[i] = base[i] + squared[i] * total
    first[...] = one[:4]
    last[...] = one[12:]
    inside(one, depth, width, most)
    for i in range(16):
        most[i] = 2.0 * one[i] - current[i] + squared[i] * most[i]


def last_kernel(most, squared, before, after, out):
    out[4:12] = most[4:12]
    for i in (0, 1, 2, 3):
        out[i] = most[i] + squared[i] * jnp.where(lax.axis_index(SLAB) == 0, 0.0, beyond(before, after, i, 16))
    for i in (12, 13, 14, 15):
        out[i] = most[i] + squared[i] * jnp.where(lax.axis_index(SLAB) == 7, 0.0, beyond(before, after, i, 16))


def on_slab(kernel, outs, *args, scratch=(), bytes_accessed=8 << 20):
    vmem = pl.BlockSpec(memory_space=pltpu.VMEM)
    return pl.pallas_call(
        kernel,
        out_shape=[jax.ShapeDtypeStruct((planes, 64, 256), jnp.float32) for planes in outs],
        in_specs=[vmem] * len(args),
        out_specs=[vmem] * len(outs),
        scratch_shapes=list(scratch),
        cost_estimate=pl.CostEstimate(flops=1 << 27, bytes_accessed=bytes_accessed, transcendentals=0),
        compiler_params=pltpu.CompilerParams(vmem_limit_bytes=20 << 20),
    )(*args)


def chip_index():
    return 4 * lax.axis_index("yh") + lax.axis_index("x")


def pack_kernel(offset, gradient, illumination, velocity, out, packed, tile, arrived, left):
    chip, c = chip_index(), lax.axis_index("c")
    half = pl.ds(pl.multiple_of(128 * lax.rem(chip, 2), 128), 128)
    parts = [pl.ds(32 * i, 32) for i in range(4)]
    reads = []
    for i, part in enumerate(parts):
        pairs = [(velocity.at[lax.div(chip, 2), part, :, half], tile.at[part])]
        for k, source in enumerate((gradient, illumination)):
            for h in range(2):
                to = packed.at[part, pl.ds(16 * k + 8 * h, 8)]
                pairs.append((source.at[part, :, pl.ds(128 * h, 128)], to))
        reads.append([pltpu.make_async_copy(a, b, arrived.at[5 * i + j]) for j, (a, b) in enumerate(pairs)])
        for copy in reads[-1]:
            copy.start()
    writes = []
    for i, part in enumerate(parts):
        for copy in reads[i]:
            copy.wait()
        upper = lax.broadcasted_iota(jnp.int32, (32, 8, 128), 1) // 4
        packed[part, 32:] = jnp.where(upper == c, tile[part], offset[0].astype(jnp.float32))
        writes.append(pltpu.make_async_copy(packed.at[part], out.at[part], left.at[i]))
        writes[-1].start()
    for copy in writes:
        copy.wait()


def pack(offsets, gradient, illumination, velocity):
    anywhere = pl.BlockSpec(memory_space=pl.ANY)
    return pl.pallas_call(
        pack_kernel,
        out_shape=jax.ShapeDtypeStruct((128, 40, 128), gradient.dtype),
        in_specs=[pl.BlockSpec(memory_space=pltpu.SMEM)] + [anywhere] * 3,
        out_specs=anywhere,
        scratch_shapes=[
            pltpu.VMEM((128, 40, 128), gradient.dtype),
            pltpu.VMEM((128, 8, 128), gradient.dtype),
            pltpu.SemaphoreType.DMA((20,)),
            pltpu.SemaphoreType.DMA((4,)),
        ],
        cost_estimate=pl.CostEstimate(flops=0, bytes_accessed=5 << 20, transcendentals=0),
        compiler_params=pltpu.CompilerParams(vmem_limit_bytes=60 << 20),
    )(
        offsets,
        gradient.reshape(128, 8, 256),
        illumination.reshape(128, 8, 256),
        velocity.reshape(4, 128, 8, 256),
    )


def model_kernel(sent, out, grad, illum, marks, arrived):
    copy = pltpu.make_async_copy(sent.at[:, 0, pl.ds(32, 8)], marks, arrived)
    copy.start()
    grad[...] = jnp.zeros_like(grad)
    illum[...] = jnp.zeros_like(illum)
    copy.wait()
    offs = [marks[shot, 4 - 4 * (shot % 2), 0].astype(jnp.int32) for shot in range(16)]
    for shot in range(16):
        grad[pl.ds(offs[shot], 8)] += sent[shot, :, :16]
        illum[pl.ds(offs[shot], 8)] += sent[shot, :, 16:32]
    for pair in range(8):
        slabs, rows = pl.ds(8 * (pair // 2), 8), pl.ds(8 * (pair % 2), 8)
        low = sent[2 * pair, :, 32:]
        high = sent[2 * pair + 1, :, 32:]
        velocity = jnp.where(lax.broadcasted_iota(jnp.int32, low.shape, 1) < 4, low, high)
        new = velocity - RATE * grad[slabs, rows] / (illum[slabs, rows] + 1.0)
        grad[slabs, rows] = new
        out[16 * pair : 16 * pair + 8, 16:] = new
        out[16 * pair + 8 : 16 * pair + 16, 16:] = new
    for shot in range(16):
        out[8 * shot : 8 * shot + 8, :16] = grad[pl.ds(offs[shot], 8)]


def update_model(sent):
    vmem = pl.BlockSpec(memory_space=pltpu.VMEM)
    return pl.pallas_call(
        model_kernel,
        out_shape=jax.ShapeDtypeStruct((128, 24, 128), sent.dtype),
        in_specs=[vmem],
        out_specs=vmem,
        scratch_shapes=[pltpu.VMEM((32, 16, 128), sent.dtype)] * 2
        + [pltpu.SMEM((16, 8, 128), sent.dtype), pltpu.SemaphoreType.DMA],
        cost_estimate=pl.CostEstimate(flops=1 << 20, bytes_accessed=4 << 20, transcendentals=0),
        compiler_params=pltpu.CompilerParams(vmem_limit_bytes=10 << 20),
    )(sent.reshape(16, 8, 40, 128))


def place_kernel(spots, *refs):
    pieces, out, sems = refs[: len(spots)], refs[-2], refs[-1]
    yh, x, c = (lax.axis_index(a) for a in SHOT)
    copies = []
    for i, (piece, (dy, dx, dc)) in enumerate(zip(pieces, spots)):
        chip = lax.rem(yh + dy, 2) * 4 + lax.rem(x + 4 - dx, 4)
        core = 0 if dc is None else lax.rem(c + dc, 2)
        planes = pl.ds(pl.multiple_of(8 * core, 8), piece.shape[0])
        lanes = pl.ds(pl.multiple_of(128 * lax.rem(chip, 2), 128), 128)
        target = out.at[lax.div(chip, 2), planes, :, lanes]
        copies.append(pltpu.make_async_copy(piece, target, sems.at[i]))
    for copy in copies:
        copy.start()
    for copy in copies:
        copy.wait()


def place_pieces(pieces, model=None):
    count = len(pieces)
    anywhere = pl.BlockSpec(memory_space=pl.ANY)
    hbm = pl.BlockSpec(memory_space=pltpu.HBM)
    rest = [] if model is None else [model]
    values = [piece[0] for piece in pieces]
    return pl.pallas_call(
        functools.partial(place_kernel, [piece[1:] for piece in pieces]),
        out_shape=jax.ShapeDtypeStruct((4, 16, 64, 256), values[0].dtype),
        in_specs=[anywhere] * count + [hbm] * len(rest),
        out_specs=hbm,
        input_output_aliases={count: 0} if rest else {},
        scratch_shapes=[pltpu.SemaphoreType.DMA((count,))],
        cost_estimate=pl.CostEstimate(flops=0, bytes_accessed=count << 19, transcendentals=0),
        compiler_params=pltpu.CompilerParams(vmem_limit_bytes=4 << 20),
    )(*values, *rest)


def gather_and_step(block, own, step, advance):
    def with_other_core(values):
        return [
            piece
            for value, dy, dx in values
            for piece in ((value, dy, dx, 0), (rotate(value, "c", 1), dy, dx, 1))
        ]

    one, two, three = (rotate(own, "x", k) for k in (1, 2, 3))
    flip = rotate(own, "yh", 1)
    most, squared, first, last = step
    around = halo(last, first)
    (one, two, three, flip), most = lax.optimization_barrier(((one, two, three, flip), most))
    second = [rotate(flip, "x", 1), rotate(flip, "x", 3), rotate(two, "yh", 1)]
    final = advance(most, squared, around)
    pieces = with_other_core([(one, 0, 1), (two, 0, 2), (three, 0, 3), (flip, 1, 0)])
    model = place_pieces([(block, 0, 0, None)] + pieces)
    second, model, final = lax.optimization_barrier((second, model, final))
    return place_pieces(with_other_core([(second[0], 1, 1), (second[1], 1, 3), (second[2], 1, 2)]), model), final


def on_device(gradient, illumination, u_prev, u_cur, velocity, offsets):
    u_prev, u_cur = u_prev[0], u_cur[0]
    c = lax.axis_index("c")

    sent = lax.all_to_all(pack(offsets, gradient, illumination, velocity), AXES, 0, 0)
    back = lax.all_to_all(update_model(sent), AXES, 0, 0)

    around = halo(u_cur[12:], u_cur[:4])
    depth, width = banded(256, 3.0 * STENCIL[0]), banded(64, 0.0)

    block = back[:, 16:]
    own = lax.dynamic_slice(block, (64 * c, 0, 0), (64, 8, 128)).reshape(8, 64, 128)
    field = pltpu.VMEM((16, 64, 256), jnp.float32)
    current, previous = u_cur, u_prev
    base, lap = on_slab(first_kernel, (16, 16), previous, current, depth, width)
    step = on_slab(
        second_kernel, (16, 16, 4, 4), back, base, lap, current, *around, depth, width, scratch=[field]
    )

    def advance(most, squared, around):
        return on_slab(last_kernel, (16,), most, squared, *around)[0]

    new_model, final = gather_and_step(block.reshape(16, 64, 128), own, tuple(step), advance)
    return new_model, final[None]


def solution(mesh):
    fine = Mesh(mesh.devices.reshape(tuple(SIZES[a] for a in AXES)), AXES)
    field = P(SHOT, SLAB, None, None)
    model = P(None, SLAB, None, None)
    return jax.shard_map(
        on_device,
        mesh=fine,
        in_specs=(field, field, field, field, model, P(SHOT)),
        out_specs=(model, field),
        check_vma=False,
    )
```

```python
import functools

import jax
import jax.numpy as jnp
import numpy as np
from jax import lax
from jax.experimental import pallas as pl
from jax.experimental.pallas import tpu as pltpu
from jax.sharding import Mesh, PartitionSpec as P

STENCIL = (-205.0 / 72.0, 8.0 / 5.0, -1.0 / 5.0, 8.0 / 315.0, -1.0 / 560.0)
RATE = 0.2
COURANT = 0.11

AXES = ("yh", "x", "c", "yl", "z")
SIZES = {"yh": 2, "x": 4, "c": 2, "yl": 2, "z": 4}
SHOT = ("yh", "x", "c")
SLAB = ("yl", "z")


def rotate(value, axis, steps):
    count = SIZES[axis]
    return lax.ppermute(value, axis, [(i, (i + steps) % count) for i in range(count)])


def banded(length, centre):
    matrix = centre * np.eye(length)
    for reach in range(1, 5):
        matrix += STENCIL[reach] * (np.eye(length, k=reach) + np.eye(length, k=-reach))
    return jnp.asarray(matrix, jnp.float32)


def halo(last, first):
    before = lax.ppermute(last, SLAB, [(i, (i + 1) % 8) for i in range(8)])
    after = lax.ppermute(first, SLAB, [((i + 1) % 8, i) for i in range(8)])
    return before, after


def dot(a, b):
    return jnp.dot(a, b, precision=lax.Precision.HIGHEST, preferred_element_type=jnp.float32)


def inside(field, depth, width, out):
    planes = field.shape[0]
    out[...] = dot(field[...].reshape(planes * 64, 256), depth[...]).reshape(planes, 64, 256)
    for i in range(planes):
        total = dot(width[...], field[i])
        for reach in range(1, 5):
            near = [field[j] for j in (i - reach, i + reach) if 0 <= j < planes]
            total += STENCIL[reach] * sum(near[1:], near[0])
        out[i] += total


def beyond(before, after, i, planes):
    if i < 4:
        return sum(STENCIL[reach] * before[4 + i - reach] for reach in range(i + 1, 5))
    low = planes - i
    return sum(STENCIL[reach] * after[reach - low] for reach in range(low, 5))


def first_kernel(previous, current, depth, width, base, lap):
    inside(current, depth, width, lap)
    base[...] = 2.0 * current[...] - previous[...]


def second_kernel(back, base, lap, current, before, after, depth, width, most, squared, first, last, one):
    for plane in range(16):
        for block in range(8):
            for half in range(2):
                value = back[8 * plane + block, 8 * half : 8 * half + 8]
                at = (plane, slice(8 * block, 8 * block + 8), slice(128 * half, 128 * half + 128))
                squared[at] = (value * COURANT) ** 2
    for i in range(16):
        total = lap[i]
        if i < 4:
            total += jnp.where(lax.axis_index(SLAB) == 0, 0.0, beyond(before, after, i, 16))
        if i >= 12:
            total += jnp.where(lax.axis_index(SLAB) == 7, 0.0, beyond(before, after, i, 16))
        one[i] = base[i] + squared[i] * total
    first[...] = one[:4]
    last[...] = one[12:]
    inside(one, depth, width, most)
    for i in range(16):
        most[i] = 2.0 * one[i] - current[i] + squared[i] * most[i]


def on_slab(kernel, outs, *args, scratch=()):
    vmem = pl.BlockSpec(memory_space=pltpu.VMEM)
    return pl.pallas_call(
        kernel,
        out_shape=[jax.ShapeDtypeStruct((planes, 64, 256), jnp.float32) for planes in outs],
        in_specs=[vmem] * len(args),
        out_specs=[vmem] * len(outs),
        scratch_shapes=list(scratch),
        cost_estimate=pl.CostEstimate(flops=0, bytes_accessed=1 << 10, transcendentals=0),
        compiler_params=pltpu.CompilerParams(vmem_limit_bytes=20 << 20),
    )(*args)


def chip_index():
    return 4 * lax.axis_index("yh") + lax.axis_index("x")


def pack_kernel(offset, gradient, illumination, velocity, out, packed, tile, arrived, left):
    chip, c = chip_index(), lax.axis_index("c")
    half = pl.ds(pl.multiple_of(128 * lax.rem(chip, 2), 128), 128)
    parts = [pl.ds(32 * i, 32) for i in range(4)]
    reads = []
    for i, part in enumerate(parts):
        pairs = [(velocity.at[lax.div(chip, 2), part, :, half], tile.at[part])]
        for k, source in enumerate((gradient, illumination)):
            for h in range(2):
                to = packed.at[part, pl.ds(16 * k + 8 * h, 8)]
                pairs.append((source.at[part, :, pl.ds(128 * h, 128)], to))
        reads.append([pltpu.make_async_copy(a, b, arrived.at[5 * i + j]) for j, (a, b) in enumerate(pairs)])
        for copy in reads[-1]:
            copy.start()
    writes = []
    for i, part in enumerate(parts):
        for copy in reads[i]:
            copy.wait()
        upper = lax.broadcasted_iota(jnp.int32, (32, 8, 128), 1) // 4
        packed[part, 32:] = jnp.where(upper == c, tile[part], offset[0].astype(jnp.float32))
        writes.append(pltpu.make_async_copy(packed.at[part], out.at[part], left.at[i]))
        writes[-1].start()
    for copy in writes:
        copy.wait()


def pack(offsets, gradient, illumination, velocity):
    anywhere = pl.BlockSpec(memory_space=pl.ANY)
    return pl.pallas_call(
        pack_kernel,
        out_shape=jax.ShapeDtypeStruct((128, 40, 128), gradient.dtype),
        in_specs=[pl.BlockSpec(memory_space=pltpu.SMEM)] + [anywhere] * 3,
        out_specs=anywhere,
        scratch_shapes=[
            pltpu.VMEM((128, 40, 128), gradient.dtype),
            pltpu.VMEM((128, 8, 128), gradient.dtype),
            pltpu.SemaphoreType.DMA((20,)),
            pltpu.SemaphoreType.DMA((4,)),
        ],
        cost_estimate=pl.CostEstimate(flops=0, bytes_accessed=5 << 20, transcendentals=0),
        compiler_params=pltpu.CompilerParams(vmem_limit_bytes=60 << 20),
    )(
        offsets,
        gradient.reshape(128, 8, 256),
        illumination.reshape(128, 8, 256),
        velocity.reshape(4, 128, 8, 256),
    )


def model_kernel(sent, out, grad, illum, marks, arrived):
    copy = pltpu.make_async_copy(sent.at[:, 0, pl.ds(32, 8)], marks, arrived)
    copy.start()
    grad[...] = jnp.zeros_like(grad)
    illum[...] = jnp.zeros_like(illum)
    copy.wait()
    offs = [marks[shot, 4 - 4 * (shot % 2), 0].astype(jnp.int32) for shot in range(16)]
    for shot in range(16):
        grad[pl.ds(offs[shot], 8)] += sent[shot, :, :16]
        illum[pl.ds(offs[shot], 8)] += sent[shot, :, 16:32]
    for pair in range(8):
        slabs, rows = pl.ds(8 * (pair // 2), 8), pl.ds(8 * (pair % 2), 8)
        low = sent[2 * pair, :, 32:]
        high = sent[2 * pair + 1, :, 32:]
        velocity = jnp.where(lax.broadcasted_iota(jnp.int32, low.shape, 1) < 4, low, high)
        new = velocity - RATE * grad[slabs, rows] / (illum[slabs, rows] + 1.0)
        grad[slabs, rows] = new
        out[16 * pair : 16 * pair + 8, 16:] = new
        out[16 * pair + 8 : 16 * pair + 16, 16:] = new
    for shot in range(16):
        out[8 * shot : 8 * shot + 8, :16] = grad[pl.ds(offs[shot], 8)]


def update_model(sent):
    vmem = pl.BlockSpec(memory_space=pltpu.VMEM)
    return pl.pallas_call(
        model_kernel,
        out_shape=jax.ShapeDtypeStruct((128, 24, 128), sent.dtype),
        in_specs=[vmem],
        out_specs=vmem,
        scratch_shapes=[pltpu.VMEM((32, 16, 128), sent.dtype)] * 2
        + [pltpu.SMEM((16, 8, 128), sent.dtype), pltpu.SemaphoreType.DMA],
        cost_estimate=pl.CostEstimate(flops=1 << 20, bytes_accessed=4 << 20, transcendentals=0),
        compiler_params=pltpu.CompilerParams(vmem_limit_bytes=10 << 20),
    )(sent.reshape(16, 8, 40, 128))


def last_kernel(spots, *refs):
    count = len(spots)
    pieces, (most, squared, before, after, model, out, ends, sems) = refs[:count], refs[count:]
    yh, x, c = (lax.axis_index(a) for a in SHOT)
    middle = pl.ds(4, 8)
    copies = [pltpu.make_async_copy(most.at[middle], out.at[middle], sems.at[count])]
    for i, (piece, (dy, dx, dc)) in enumerate(zip(pieces, spots)):
        chip = lax.rem(yh + dy, 2) * 4 + lax.rem(x + 4 - dx, 4)
        core = 0 if dc is None else lax.rem(c + dc, 2)
        planes = pl.ds(pl.multiple_of(8 * core, 8), piece.shape[0])
        lanes = pl.ds(pl.multiple_of(128 * lax.rem(chip, 2), 128), 128)
        target = model.at[lax.div(chip, 2), planes, :, lanes]
        copies.append(pltpu.make_async_copy(piece, target, sems.at[i]))
    for copy in copies:
        copy.start()
    slab = lax.axis_index(SLAB)
    for i in range(4):
        ends[i] = most[i] + squared[i] * jnp.where(slab == 0, 0.0, beyond(before, after, i, 16))
        j = 12 + i
        ends[4 + i] = most[j] + squared[j] * jnp.where(slab == 7, 0.0, beyond(before, after, j, 16))
    for i in range(2):
        edge = pltpu.make_async_copy(ends.at[pl.ds(4 * i, 4)], out.at[pl.ds(12 * i, 4)], sems.at[count + 1 + i])
        edge.start()
        copies.append(edge)
    for copy in copies:
        copy.wait()


def finish(pieces, most, squared, before, after):
    count = len(pieces)
    anywhere = pl.BlockSpec(memory_space=pl.ANY)
    vmem = pl.BlockSpec(memory_space=pltpu.VMEM)
    hbm = pl.BlockSpec(memory_space=pltpu.HBM)
    return pl.pallas_call(
        functools.partial(last_kernel, [piece[1:] for piece in pieces]),
        out_shape=[
            jax.ShapeDtypeStruct((4, 16, 64, 256), most.dtype),
            jax.ShapeDtypeStruct((16, 64, 256), most.dtype),
        ],
        in_specs=[anywhere] * count + [vmem] * 4,
        out_specs=[hbm] * 2,
        scratch_shapes=[pltpu.VMEM((8, 64, 256), most.dtype), pltpu.SemaphoreType.DMA((count + 3,))],
        cost_estimate=pl.CostEstimate(flops=0, bytes_accessed=10 << 20, transcendentals=0),
        compiler_params=pltpu.CompilerParams(vmem_limit_bytes=8 << 20),
    )(*[piece[0] for piece in pieces], most, squared, before, after)


def gather_and_step(block, own, step):
    def with_other_core(values):
        return [
            piece
            for value, dy, dx in values
            for piece in ((value, dy, dx, 0), (rotate(value, "c", 1), dy, dx, 1))
        ]

    one, two, three = (rotate(own, "x", k) for k in (1, 2, 3))
    flip = rotate(own, "yh", 1)
    most, squared, first, last = step
    around = halo(last, first)
    (one, two, three, flip), most = lax.optimization_barrier(((one, two, three, flip), most))
    second = [rotate(flip, "x", 1), rotate(flip, "x", 3), rotate(two, "yh", 1)]
    (one, two, three, flip), around = lax.optimization_barrier(((one, two, three, flip), around))
    pieces = [(block, 0, 0, None)]
    pieces += with_other_core([(one, 0, 1), (two, 0, 2), (three, 0, 3), (flip, 1, 0)])
    pieces += with_other_core([(second[0], 1, 1), (second[1], 1, 3), (second[2], 1, 2)])
    return finish(pieces, most, squared, *around)


def on_device(gradient, illumination, u_prev, u_cur, velocity, offsets):
    u_prev, u_cur = u_prev[0], u_cur[0]
    c = lax.axis_index("c")

    sent = lax.all_to_all(pack(offsets, gradient, illumination, velocity), AXES, 0, 0)
    back = lax.all_to_all(update_model(sent), AXES, 0, 0)

    around = halo(u_cur[12:], u_cur[:4])
    depth, width = banded(256, 3.0 * STENCIL[0]), banded(64, 0.0)

    block = back[:, 16:]
    own = lax.dynamic_slice(block, (64 * c, 0, 0), (64, 8, 128)).reshape(8, 64, 128)
    field = pltpu.VMEM((16, 64, 256), jnp.float32)
    current, previous = u_cur, u_prev
    base, lap = on_slab(first_kernel, (16, 16), previous, current, depth, width)
    step = on_slab(
        second_kernel, (16, 16, 4, 4), back, base, lap, current, *around, depth, width, scratch=[field]
    )

    new_model, final = gather_and_step(block.reshape(16, 64, 128), own, tuple(step))
    return new_model, final[None]


def solution(mesh):
    fine = Mesh(mesh.devices.reshape(tuple(SIZES[a] for a in AXES)), AXES)
    field = P(SHOT, SLAB, None, None)
    model = P(None, SLAB, None, None)
    return jax.shard_map(
        on_device,
        mesh=fine,
        in_specs=(field, field, field, field, model, P(SHOT)),
        out_specs=(model, field),
        check_vma=False,
    )
```

```python
import functools

import jax
import jax.numpy as jnp
import numpy as np
from jax import lax
from jax.experimental import pallas as pl
from jax.experimental.pallas import tpu as pltpu
from jax.sharding import Mesh, PartitionSpec as P

STENCIL = (-205.0 / 72.0, 8.0 / 5.0, -1.0 / 5.0, 8.0 / 315.0, -1.0 / 560.0)
RATE = 0.2
COURANT = 0.11

AXES = ("yh", "x", "c", "yl", "z")
SIZES = {"yh": 2, "x": 4, "c": 2, "yl": 2, "z": 4}
SHOT = ("yh", "x", "c")
SLAB = ("yl", "z")


def rotate(value, axis, steps):
    count = SIZES[axis]
    return lax.ppermute(value, axis, [(i, (i + steps) % count) for i in range(count)])


def banded(length, centre):
    matrix = centre * np.eye(length)
    for reach in range(1, 5):
        matrix += STENCIL[reach] * (np.eye(length, k=reach) + np.eye(length, k=-reach))
    return jnp.asarray(matrix, jnp.float32)


def halo(last, first):
    before = lax.ppermute(last, SLAB, [(i, (i + 1) % 8) for i in range(8)])
    after = lax.ppermute(first, SLAB, [((i + 1) % 8, i) for i in range(8)])
    return before, after


def dot(a, b):
    return jnp.dot(a, b, precision=lax.Precision.HIGHEST, preferred_element_type=jnp.float32)


def inside(field, depth, width, out):
    planes = field.shape[0]
    out[...] = dot(field[...].reshape(planes * 64, 256), depth[...]).reshape(planes, 64, 256)
    for i in range(planes):
        total = dot(width[...], field[i])
        for reach in range(1, 5):
            near = [field[j] for j in (i - reach, i + reach) if 0 <= j < planes]
            total += STENCIL[reach] * sum(near[1:], near[0])
        out[i] += total


def beyond(before, after, i, planes):
    if i < 4:
        return sum(STENCIL[reach] * before[4 + i - reach] for reach in range(i + 1, 5))
    low = planes - i
    return sum(STENCIL[reach] * after[reach - low] for reach in range(low, 5))


def first_kernel(previous, current, depth, width, base, lap):
    inside(current, depth, width, lap)
    base[...] = 2.0 * current[...] - previous[...]


def second_kernel(back, base, lap, current, before, after, depth, width, most, squared, first, last, one):
    for plane in range(16):
        for block in range(8):
            for half in range(2):
                value = back[8 * plane + block, 8 * half : 8 * half + 8]
                at = (plane, slice(8 * block, 8 * block + 8), slice(128 * half, 128 * half + 128))
                squared[at] = (value * COURANT) ** 2
    for i in range(16):
        total = lap[i]
        if i < 4:
            total += jnp.where(lax.axis_index(SLAB) == 0, 0.0, beyond(before, after, i, 16))
        if i >= 12:
            total += jnp.where(lax.axis_index(SLAB) == 7, 0.0, beyond(before, after, i, 16))
        one[i] = base[i] + squared[i] * total
    first[...] = one[:4]
    last[...] = one[12:]
    inside(one, depth, width, most)
    for i in range(16):
        most[i] = 2.0 * one[i] - current[i] + squared[i] * most[i]


def on_slab(kernel, outs, *args, scratch=()):
    vmem = pl.BlockSpec(memory_space=pltpu.VMEM)
    return pl.pallas_call(
        kernel,
        out_shape=[jax.ShapeDtypeStruct((planes, 64, 256), jnp.float32) for planes in outs],
        in_specs=[vmem] * len(args),
        out_specs=[vmem] * len(outs),
        scratch_shapes=list(scratch),
        cost_estimate=pl.CostEstimate(flops=0, bytes_accessed=1 << 10, transcendentals=0),
        compiler_params=pltpu.CompilerParams(vmem_limit_bytes=20 << 20),
    )(*args)


def chip_index():
    return 4 * lax.axis_index("yh") + lax.axis_index("x")


def pack_kernel(offset, gradient, illumination, velocity, out, packed, tile, arrived, left):
    chip, c = chip_index(), lax.axis_index("c")
    half = pl.ds(pl.multiple_of(128 * lax.rem(chip, 2), 128), 128)
    parts = [pl.ds(16 * i, 16) for i in range(8)]
    reads = []
    for i, part in enumerate(parts):
        pairs = [(velocity.at[lax.div(chip, 2), part, :, half], tile.at[part])]
        for k, source in enumerate((gradient, illumination)):
            for h in range(2):
                to = packed.at[part, pl.ds(16 * k + 8 * h, 8)]
                pairs.append((source.at[part, :, pl.ds(128 * h, 128)], to))
        reads.append([pltpu.make_async_copy(a, b, arrived.at[5 * i + j]) for j, (a, b) in enumerate(pairs)])
        for copy in reads[-1]:
            copy.start()
    writes = []
    for i, part in enumerate(parts):
        for copy in reads[i]:
            copy.wait()
        upper = lax.broadcasted_iota(jnp.int32, (16, 8, 128), 1) // 4
        packed[part, 32:] = jnp.where(upper == c, tile[part], offset[0].astype(jnp.float32))
        writes.append(pltpu.make_async_copy(packed.at[part], out.at[part], left.at[i]))
        writes[-1].start()
    for copy in writes:
        copy.wait()


def pack(offsets, gradient, illumination, velocity):
    anywhere = pl.BlockSpec(memory_space=pl.ANY)
    return pl.pallas_call(
        pack_kernel,
        out_shape=jax.ShapeDtypeStruct((128, 40, 128), gradient.dtype),
        in_specs=[pl.BlockSpec(memory_space=pltpu.SMEM)] + [anywhere] * 3,
        out_specs=anywhere,
        scratch_shapes=[
            pltpu.VMEM((128, 40, 128), gradient.dtype),
            pltpu.VMEM((128, 8, 128), gradient.dtype),
            pltpu.SemaphoreType.DMA((40,)),
            pltpu.SemaphoreType.DMA((8,)),
        ],
        cost_estimate=pl.CostEstimate(flops=0, bytes_accessed=5 << 20, transcendentals=0),
        compiler_params=pltpu.CompilerParams(vmem_limit_bytes=60 << 20),
    )(
        offsets,
        gradient.reshape(128, 8, 256),
        illumination.reshape(128, 8, 256),
        velocity.reshape(4, 128, 8, 256),
    )


def model_kernel(sent, out, grad, illum):
    grad[...] = jnp.zeros_like(grad)
    illum[...] = jnp.zeros_like(illum)
    offs = []
    for shot in range(16):
        row = 36 - 4 * (shot % 2)
        offs.append(jnp.max(sent[shot, 0, row : row + 1]).astype(jnp.int32))
    for shot in range(16):
        grad[pl.ds(offs[shot], 8)] += sent[shot, :, :16]
        illum[pl.ds(offs[shot], 8)] += sent[shot, :, 16:32]
    for pair in range(8):
        slabs, rows = pl.ds(8 * (pair // 2), 8), pl.ds(8 * (pair % 2), 8)
        low = sent[2 * pair, :, 32:]
        high = sent[2 * pair + 1, :, 32:]
        velocity = jnp.where(lax.broadcasted_iota(jnp.int32, low.shape, 1) < 4, low, high)
        new = velocity - RATE * grad[slabs, rows] / (illum[slabs, rows] + 1.0)
        grad[slabs, rows] = new
        out[16 * pair : 16 * pair + 8, 16:] = new
        out[16 * pair + 8 : 16 * pair + 16, 16:] = new
    for shot in range(16):
        out[8 * shot : 8 * shot + 8, :16] = grad[pl.ds(offs[shot], 8)]


def update_model(sent):
    vmem = pl.BlockSpec(memory_space=pltpu.VMEM)
    return pl.pallas_call(
        model_kernel,
        out_shape=jax.ShapeDtypeStruct((128, 24, 128), sent.dtype),
        in_specs=[vmem],
        out_specs=vmem,
        scratch_shapes=[pltpu.VMEM((32, 16, 128), sent.dtype)] * 2,
        cost_estimate=pl.CostEstimate(flops=1 << 20, bytes_accessed=4 << 20, transcendentals=0),
        compiler_params=pltpu.CompilerParams(vmem_limit_bytes=10 << 20),
    )(sent.reshape(16, 8, 40, 128))


def last_kernel(spots, *refs):
    count = len(spots)
    pieces, (most, squared, before, after, model, out, ends, sems) = refs[:count], refs[count:]
    yh, x, c = (lax.axis_index(a) for a in SHOT)
    middle = pl.ds(4, 8)
    copies = [pltpu.make_async_copy(most.at[middle], out.at[middle], sems.at[count])]
    for i, (piece, (dy, dx, dc)) in enumerate(zip(pieces, spots)):
        chip = lax.rem(yh + dy, 2) * 4 + lax.rem(x + 4 - dx, 4)
        core = 0 if dc is None else lax.rem(c + dc, 2)
        planes = pl.ds(pl.multiple_of(8 * core, 8), piece.shape[0])
        lanes = pl.ds(pl.multiple_of(128 * lax.rem(chip, 2), 128), 128)
        target = model.at[lax.div(chip, 2), planes, :, lanes]
        copies.append(pltpu.make_async_copy(piece, target, sems.at[i]))
    for copy in copies:
        copy.start()
    slab = lax.axis_index(SLAB)
    for i in range(4):
        ends[i] = most[i] + squared[i] * jnp.where(slab == 0, 0.0, beyond(before, after, i, 16))
        j = 12 + i
        ends[4 + i] = most[j] + squared[j] * jnp.where(slab == 7, 0.0, beyond(before, after, j, 16))
    for i in range(2):
        edge = pltpu.make_async_copy(ends.at[pl.ds(4 * i, 4)], out.at[pl.ds(12 * i, 4)], sems.at[count + 1 + i])
        edge.start()
        copies.append(edge)
    for copy in copies:
        copy.wait()


def finish(pieces, most, squared, before, after):
    count = len(pieces)
    anywhere = pl.BlockSpec(memory_space=pl.ANY)
    vmem = pl.BlockSpec(memory_space=pltpu.VMEM)
    hbm = pl.BlockSpec(memory_space=pltpu.HBM)
    return pl.pallas_call(
        functools.partial(last_kernel, [piece[1:] for piece in pieces]),
        out_shape=[
            jax.ShapeDtypeStruct((4, 16, 64, 256), most.dtype),
            jax.ShapeDtypeStruct((16, 64, 256), most.dtype),
        ],
        in_specs=[anywhere] * count + [vmem] * 4,
        out_specs=[hbm] * 2,
        scratch_shapes=[pltpu.VMEM((8, 64, 256), most.dtype), pltpu.SemaphoreType.DMA((count + 3,))],
        cost_estimate=pl.CostEstimate(flops=0, bytes_accessed=10 << 20, transcendentals=0),
        compiler_params=pltpu.CompilerParams(vmem_limit_bytes=8 << 20),
    )(*[piece[0] for piece in pieces], most, squared, before, after)


def gather_and_step(block, own, step):
    def with_other_core(values):
        return [
            piece
            for value, dy, dx in values
            for piece in ((value, dy, dx, 0), (rotate(value, "c", 1), dy, dx, 1))
        ]

    one, two, three = (rotate(own, "x", k) for k in (1, 2, 3))
    flip = rotate(own, "yh", 1)
    most, squared, first, last = step
    around = halo(last, first)
    (one, two, three, flip), most = lax.optimization_barrier(((one, two, three, flip), most))
    second = [rotate(flip, "x", 1), rotate(flip, "x", 3), rotate(two, "yh", 1)]
    (one, two, three, flip), around = lax.optimization_barrier(((one, two, three, flip), around))
    pieces = [(block, 0, 0, None)]
    pieces += with_other_core([(one, 0, 1), (two, 0, 2), (three, 0, 3), (flip, 1, 0)])
    pieces += with_other_core([(second[0], 1, 1), (second[1], 1, 3), (second[2], 1, 2)])
    return finish(pieces, most, squared, *around)


def on_device(gradient, illumination, u_prev, u_cur, velocity, offsets):
    u_prev, u_cur = u_prev[0], u_cur[0]
    c = lax.axis_index("c")

    sent = lax.all_to_all(pack(offsets, gradient, illumination, velocity), AXES, 0, 0)
    back = lax.all_to_all(update_model(sent), AXES, 0, 0)

    around = halo(u_cur[12:], u_cur[:4])
    depth, width = banded(256, 3.0 * STENCIL[0]), banded(64, 0.0)

    block = back[:, 16:]
    own = lax.dynamic_slice(block, (64 * c, 0, 0), (64, 8, 128)).reshape(8, 64, 128)
    field = pltpu.VMEM((16, 64, 256), jnp.float32)
    current, previous = u_cur, u_prev
    base, lap = on_slab(first_kernel, (16, 16), previous, current, depth, width)
    step = on_slab(
        second_kernel, (16, 16, 4, 4), back, base, lap, current, *around, depth, width, scratch=[field]
    )

    new_model, final = gather_and_step(block.reshape(16, 64, 128), own, tuple(step))
    return new_model, final[None]


def solution(mesh):
    fine = Mesh(mesh.devices.reshape(tuple(SIZES[a] for a in AXES)), AXES)
    field = P(SHOT, SLAB, None, None)
    model = P(None, SLAB, None, None)
    return jax.shard_map(
        on_device,
        mesh=fine,
        in_specs=(field, field, field, field, model, P(SHOT)),
        out_specs=(model, field),
        check_vma=False,
    )
```
